32 devices in a mesh: req: 16 (over z, y, x), tp: 2 (over core).
Axes of the slice: x: 2, y: 2, z: 4, core: 2. Of those that a mesh axis runs over, the one named last changes fastest.
Arguments:
- suffix_tokens: bfloat16 [256, 112, 2880], P('req'), may hold values from -40 to 40
- route_lengths: int32 [16, 16], replicated, may hold values from 1 to 112, 768 in all within a row
- dest_perm: int32 [16, 16], replicated, may hold values from 0 to 15, each once within a row
- attach_points: int32 [256], replicated, may hold values from 256 to 8192
- prefix_cache: bfloat16 [64, 128, 8, 128], P('req', None, 'tp'), may hold values from -120 to 120
- block_of_slot: int32 [64], replicated, may hold values from 0 to 63, each once
- sink_logits: float32 [64], P('tp'), may hold values from 0 to 6
- attn_gain: bfloat16 [2880], replicated, may hold values from 0.099609375 to 1.8984375
- w_query: bfloat16 [2880, 4096], P(None, 'tp'), may hold values from -0.109375 to 0.109375
- w_keyval: bfloat16 [2880, 8, 128], P(None, 'tp'), may hold values from -0.109375 to 0.109375
- w_out: bfloat16 [4096, 2880], P('tp'), may hold values from -0.09375 to 0.09375
- mlp_gain: bfloat16 [2880], replicated, may hold values from 0.099609375 to 1.8984375
- w_gate: bfloat16 [2880, 2880], P(None, 'tp'), may hold values from -0.109375 to 0.109375
- w_up: bfloat16 [2880, 2880], P(None, 'tp'), may hold values from -0.109375 to 0.109375
- w_down: bfloat16 [2880, 2880], P('tp'), may hold values from -0.109375 to 0.109375
Outputs:
- layer_out: bfloat16 [256, 112, 2880], P('req', None, 'tp')
The draws below stay inside these ranges and needn't reach their ends.
Inputs may be any that keep to these rules, and one draw needn't show every extreme that they name: `route_lengths`: each row sums to 768, and the largest entry of each row is 112. `dest_perm`: each row is a permutation of the devices of req. `block_of_slot`: a permutation.
All inputs are finite; a program needn't handle non-finite values.
Results may differ from the reference program's by a relative error of at most 0.013.
Values may be sent and summed in bfloat16 or wider, within the bound.
A program may use at most 256 MiB of HBM per device.

```python
import math
import jax
import jax.numpy as jnp
import numpy as np
from jax import lax

D = 2880
HQ = 64
KVH = 8
HD = 64
FF = 2880
WINDOW = 128
PREFIX = 8192
PBLK = 128
MAXLEN = 112
CAP = 768
REQUESTS = 256
PBLOCKS = 64
N_REQ = 16
N_TP = 2


def draw_suffix_tokens(key, part):
    column_key, row_key, base_key = jax.random.split(key, 3)
    full_shape = (REQUESTS, MAXLEN, D)
    position_ramp = jnp.arange(D).astype(jnp.float32) / (D - 1)
    columns = jnp.exp(math.log(3.0) * (position_ramp - 0.5)) * jax.random.uniform(column_key, (D,), minval=0.7, maxval=1.3)
    row_scale = jnp.exp(jax.random.uniform(row_key, (REQUESTS, MAXLEN, 1), minval=math.log(0.3), maxval=math.log(3.0)))
    base_values = jax.random.normal(base_key, full_shape)
    return jnp.clip(base_values * row_scale * columns, -40.0, 40.0).astype(jnp.bfloat16)


def draw_prefix_cache(key, part):
    value_key, boost_key = jax.random.split(key, 2)
    full_shape = (PBLOCKS, PBLK, KVH, 2 * HD)
    base_values = jax.random.normal(value_key, full_shape)
    row_boost = jnp.exp(jax.random.uniform(boost_key, (PBLOCKS, PBLK, KVH, 1), minval=math.log(0.5), maxval=math.log(2.0)))
    key_lanes = jnp.arange(2 * HD) < HD
    return jnp.clip(jnp.where(key_lanes, base_values * row_boost, base_values), -120.0, 120.0).astype(jnp.bfloat16)


def set_ends(drawn, stream_key, least, top_value):
    extent = drawn.shape
    spot = [jax.random.randint(jax.random.fold_in(stream_key, axis), (), 0, extent[axis]) for axis in range(len(extent))]
    drawn = drawn.at[tuple(spot)].set(least)
    longest = extent.index(max(extent))
    spot[longest] = (spot[longest] + 1) % extent[longest]
    return drawn.at[tuple(spot)].set(top_value)


def steps_of(own_key, shape, cuts, least, top_value):
    level, own = 1.0, jax.random.fold_in(own_key, 6)
    for axis_at, shards_of in cuts:
        draws = jnp.exp(jax.random.uniform(jax.random.fold_in(own, axis_at), (shards_of,), jnp.float32, least / len(cuts), top_value / len(cuts)))
        level = level * jnp.repeat(draws, shape[axis_at] // shards_of).reshape([-1 if axis == axis_at else 1 for axis in range(len(shape))])
    return level


def profile(number_of, total, bound, slope):
    portions = [(1 << 20) // math.isqrt(standing ** slope) + 1 for standing in range(2, number_of + 1)]
    surplus, counts = total - bound - (number_of - 1), [1] * (number_of - 1)
    while surplus > 0:
        free = [i for i in range(number_of - 1) if counts[i] < bound]
        whole, left = sum([portions[i] for i in free]), surplus
        for i in free:
            more = min(bound - counts[i], max(1, left * portions[i] // whole), surplus)
            counts[i] = counts[i] + more
            surplus = surplus - more
    return np.array([bound] + counts)


def uneven(own_key, amount, total, reach, lean):
    if amount == 2:
        one = jax.random.randint(own_key, (), max(1, total - reach), min(reach, total - 1) + 1)
        return jnp.stack([one, total - one])
    sizes = jnp.asarray(profile(amount, total, reach, lean), jnp.int32)
    twos = (amount - 1) // 2
    giver, taker = sizes[1:1 + 2 * twos:2], sizes[2:2 + 2 * twos:2]
    margin = jnp.minimum(giver - 1, reach - taker)
    passed = jax.random.randint(jax.random.fold_in(own_key, 1), (twos,), 0, 1 << 20) % (margin + 1)
    sizes = sizes.at[1:1 + 2 * twos:2].set(giver - passed).at[2:2 + 2 * twos:2].set(taker + passed)
    return sizes[jax.random.permutation(jax.random.fold_in(own_key, 2), amount)]


def bell_draw(key, dims, scale, bound, cuts=(), held_as=jnp.bfloat16):
    entries = scale * jax.random.normal(key, dims, jnp.float32)
    if cuts:
        entries = entries * steps_of(key, dims, cuts, -0.22, 0.18)
    return jnp.clip(entries, -bound, bound).astype(held_as)


def setup_inputs(seed: int = 0) -> dict:
    streams_of = jax.random.split(jax.random.key(seed), 16)
    return {
        "suffix_tokens": draw_suffix_tokens(jax.random.fold_in(streams_of[15], 71), 0),
        "route_lengths": jax.vmap(lambda own: uneven(own, N_REQ, CAP, MAXLEN, 2))(jax.random.split(streams_of[1], N_REQ)).reshape((N_REQ, N_REQ)).astype(jnp.int32),
        "dest_perm": jax.vmap(lambda own: jax.random.permutation(own, N_REQ))(jax.random.split(streams_of[2], N_REQ)).reshape((N_REQ, N_REQ)).astype(jnp.int32),
        "attach_points": set_ends(jax.random.randint(streams_of[3], (REQUESTS,), 2 * WINDOW, PREFIX + 1), jax.random.fold_in(streams_of[3], 1), 2 * WINDOW, PREFIX).astype(jnp.int32),
        "prefix_cache": draw_prefix_cache(jax.random.fold_in(streams_of[15], 71), 0),
        "block_of_slot": jax.random.permutation(streams_of[5], PBLOCKS).astype(jnp.int32),
        "sink_logits": jnp.clip(6.0 * jax.random.uniform(streams_of[6], (HQ,), jnp.float32) ** steps_of(streams_of[6], (HQ,), ((0, 2),), -0.2, 0.2), 0.0, 6.0),
        "attn_gain": jnp.clip(1.0 + 0.18 * jax.random.normal(streams_of[7], (D,), jnp.float32), 0.099609375, 1.8984375).astype(jnp.bfloat16),
        "w_query": bell_draw(streams_of[8], (D, HQ * HD), D ** -0.5, 0.109375, ((1, 2),)),
        "w_keyval": bell_draw(streams_of[9], (D, KVH, 2 * HD), D ** -0.5, 0.109375, ((1, 2),)),
        "w_out": bell_draw(streams_of[10], (HQ * HD, D), (HQ * HD) ** -0.5, 0.09375, ((0, 2),)),
        "mlp_gain": jnp.clip(1.0 + 0.18 * jax.random.normal(streams_of[11], (D,), jnp.float32), 0.099609375, 1.8984375).astype(jnp.bfloat16),
        "w_gate": bell_draw(streams_of[12], (D, FF), D ** -0.5, 0.109375, ((1, 2),)),
        "w_up": bell_draw(streams_of[13], (D, FF), D ** -0.5, 0.109375, ((1, 2),)),
        "w_down": bell_draw(streams_of[14], (FF, D), FF ** -0.5, 0.109375, ((0, 2),)),
    }


ROPE_BASE = 150000.0
EPSILON = 1e-05

def norm_rows(inputs, gains):
    widened = inputs.astype(jnp.float32)
    factor = lax.rsqrt(lax.optimization_barrier(jnp.mean(widened * widened, axis=-1, keepdims=True)) + EPSILON)
    return (widened * factor * gains.astype(jnp.float32)).astype(jnp.bfloat16)

def rotate(vectors, positions):
    half_dim = vectors.shape[-1] // 2
    frequency = ROPE_BASE ** (-(jnp.arange(half_dim).astype(jnp.float32) * 2.0 / vectors.shape[-1]))
    angles = positions.astype(jnp.float32)[:, None, None] * frequency
    cosine = jnp.cos(angles)
    sine_part = jnp.sin(angles)
    first_half = vectors[..., :half_dim]
    second = vectors[..., half_dim:]
    return jnp.concatenate([first_half * cosine - second * sine_part, second * cosine + first_half * sine_part], axis=-1)

def grouped_product(left, right, groups):
    width_part = left.shape[1] // groups
    summed = jnp.zeros((left.shape[0], right.shape[1]), jnp.float32)
    for column_group in range(groups):
        lower = column_group * width_part
        piece_sum = jnp.dot(left[:, lower:lower + width_part], right[lower:lower + width_part], preferred_element_type=jnp.float32)
        summed = summed + lax.optimization_barrier(piece_sum.astype(jnp.bfloat16)).astype(jnp.float32)
    return summed

def reference(suffix_tokens, route_lengths, dest_perm, attach_points, prefix_cache, block_of_slot, sink_logits, attn_gain, w_query, w_keyval, w_out, mlp_gain, w_gate, w_up, w_down):
    peers = route_lengths.shape[0]
    requests, slot_length, features = suffix_tokens.shape
    query_heads = sink_logits.shape[0]
    value_heads = w_keyval.shape[1]
    head_dim = w_keyval.shape[2] // 2
    group_size = query_heads // value_heads
    lengths = route_lengths[dest_perm, jnp.arange(peers)[:, None]].reshape(requests).astype(jnp.int32)
    live_total = peers * CAP
    run_ends = jnp.cumsum(lengths).astype(jnp.int32)
    starts = run_ends - lengths
    packed_ids = jnp.arange(live_total).astype(jnp.int32)
    source_of = lax.optimization_barrier(jnp.sum((run_ends[None, :] <= packed_ids[:, None]).astype(jnp.int32), axis=1))
    token_index = packed_ids - starts[source_of]
    positions = attach_points[source_of] + token_index
    input_rows = suffix_tokens[source_of, token_index]
    normed_in = norm_rows(input_rows, attn_gain)
    queries = jnp.dot(normed_in, w_query, preferred_element_type=jnp.float32).reshape(live_total, query_heads, head_dim)
    queries = rotate(queries, positions).astype(jnp.bfloat16)
    paired = jnp.dot(normed_in, w_keyval.reshape(features, -1), preferred_element_type=jnp.float32).reshape(live_total, value_heads, 2 * head_dim)
    rotated = rotate(paired[..., :head_dim], positions)
    paired = jnp.concatenate([rotated, paired[..., head_dim:]], axis=-1).astype(jnp.bfloat16)
    slot_steps = jnp.arange(slot_length).astype(jnp.int32)
    slot_source = jnp.clip(starts[:, None] + slot_steps[None, :], 0, live_total - 1)
    query_slots = queries[slot_source]
    paired_slots = paired[slot_source]
    prefix = jnp.zeros_like(prefix_cache).at[block_of_slot].set(prefix_cache).reshape(-1, value_heads, 2 * head_dim)
    sink_bias = sink_logits.astype(jnp.float32).reshape(value_heads, group_size)[:, :, None, None]
    tail_steps = jnp.arange(WINDOW)
    allowed = jnp.concatenate([tail_steps[None, :] > slot_steps[:, None], slot_steps[None, :] <= slot_steps[:, None]], axis=1)

    def one_request(request_data):
        query_block, paired_block, attach = request_data
        tail_rows = lax.dynamic_slice_in_dim(prefix, (attach - WINDOW).astype(jnp.int32), WINDOW, 0)
        all_keys = jnp.concatenate([tail_rows, paired_block], axis=0).astype(jnp.float32)
        grouped_query = query_block.reshape(slot_length, value_heads, group_size, head_dim).astype(jnp.float32)
        scores = jnp.einsum('tkgd,skd->kgts', grouped_query, all_keys[..., :head_dim]) * head_dim ** (-0.5)
        scores = jnp.where(allowed, scores, -jnp.inf)
        largest = jnp.maximum(lax.optimization_barrier(jnp.max(scores, axis=-1, keepdims=True)), sink_bias)
        weights = jnp.exp(scores - largest)
        total = lax.optimization_barrier(jnp.sum(weights, axis=-1, keepdims=True)) + jnp.exp(sink_bias - largest)
        weights = (weights / total).astype(jnp.bfloat16)
        mixed = jnp.einsum('kgts,skd->tkgd', weights.astype(jnp.float32), all_keys[..., head_dim:])
        return mixed.astype(jnp.bfloat16).reshape(slot_length, query_heads * head_dim)
    attended_slots = lax.map(one_request, (query_slots, paired_slots, attach_points))
    attended = attended_slots[source_of, token_index]
    proj = grouped_product(attended, w_out, N_TP)
    residual = (input_rows.astype(jnp.float32) + proj).astype(jnp.bfloat16)
    normed_mid = norm_rows(residual, mlp_gain)
    gate_proj = jnp.dot(normed_mid, w_gate, preferred_element_type=jnp.float32)
    up_proj = jnp.dot(normed_mid, w_up, preferred_element_type=jnp.float32)
    hidden = (jax.nn.silu(gate_proj) * up_proj).astype(jnp.bfloat16)
    down_sum = grouped_product(hidden, w_down, N_TP)
    out_rows = (residual.astype(jnp.float32) + down_sum).astype(jnp.bfloat16)
    return jnp.zeros((requests, slot_length, features), jnp.bfloat16).at[source_of, token_index].set(out_rows)
```

```python
import jax
import jax.numpy as jnp
from jax import lax
from jax.experimental import pallas as pl
from jax.experimental.pallas import tpu as pltpu
from jax.sharding import PartitionSpec as P

WINDOW = 128
CAP = 768


ROPE_BASE = 150000.0
EPSILON = 1e-05


def norm_rows(inputs, gains):
    widened = inputs.astype(jnp.float32)
    factor = lax.rsqrt(jnp.mean(widened * widened, axis=-1, keepdims=True) + EPSILON)
    return (widened * factor * gains.astype(jnp.float32)).astype(jnp.bfloat16)


CHUNK = 32
ALIGN = 8


def swap_halves(tile, lane):
    return jnp.where(lane % 64 < 32, pltpu.roll(tile, 96, 1), pltpu.roll(tile, 32, 1))


def attend_kernel(
    home_ref, offset_ref, start_ref, length_ref,
    query_ref, paired_ref, cosine_ref, sine_ref, sink_ref, prefix_ref,
    out_ref, blocks, tables, mixed, sems,
):
    peers = start_ref.shape[0]
    rows = query_ref.shape[0]
    heads = paired_ref.shape[1] // 128
    group_tiles = query_ref.shape[1] // 128 // heads

    def block_copy(n, half):
        return pltpu.make_async_copy(
            prefix_ref.at[home_ref[n, half]],
            blocks.at[n, pl.ds(half * WINDOW, WINDOW)],
            sems.at[n, half],
        )

    for n in range(peers):
        for half in range(2):
            block_copy(n, half).start()
    mixed[...] = jnp.zeros_like(mixed)

    lane = lax.broadcasted_iota(jnp.int32, (WINDOW, 128), 1)
    low = lane < 64

    def one_request(n, carry):
        start = pl.multiple_of(start_ref[n], ALIGN)
        length = length_ref[n]
        own = pl.multiple_of(jnp.minimum(start, rows - WINDOW), ALIGN)
        block_copy(n, 0).wait()
        block_copy(n, 1).wait()
        shift = (2 * WINDOW - offset_ref[n]) % (2 * WINDOW)
        cosine = cosine_ref[pl.ds(own, WINDOW), :]
        sine = sine_ref[pl.ds(own, WINDOW), :]
        for k in range(heads):
            columns = slice(k * 128, (k + 1) * 128)
            both = blocks[n, :, columns].astype(jnp.float32)
            fetched = pltpu.roll(both, shift, 0)[:WINDOW]
            fresh = paired_ref[pl.ds(own, WINDOW), columns]
            turned = fresh * cosine + swap_halves(fresh, lane) * sine
            fresh = jnp.where(low, turned, fresh)
            for part, tile in enumerate((fetched, fresh)):
                spot = slice(part * WINDOW, (part + 1) * WINDOW)
                moved = pltpu.roll(tile, 64, 1)
                tables[k, 0, spot] = jnp.where(low, tile, 0.0).astype(jnp.bfloat16)
                tables[k, 1, spot] = jnp.where(low, 0.0, moved).astype(jnp.bfloat16)
                tables[k, 2, spot] = jnp.where(low, moved, 0.0).astype(jnp.bfloat16)
                tables[k, 3, spot] = jnp.where(low, 0.0, tile).astype(jnp.bfloat16)

        shape = (group_tiles * CHUNK, 2 * WINDOW)
        step = lax.broadcasted_iota(jnp.int32, shape, 0) % CHUNK
        column = lax.broadcasted_iota(jnp.int32, shape, 1)
        own_step = column - WINDOW + (own - start)
        chunk_lane = lax.broadcasted_iota(jnp.int32, (CHUNK, 128), 1)

        def one_chunk(c, carry):
            first = pl.multiple_of(start + c * CHUNK, ALIGN)
            token = step + c * CHUNK
            allowed = ((column < WINDOW) & (column > token)) | (
                (column >= WINDOW) & (own_step >= 0) & (own_step <= token)
            )
            cosine = cosine_ref[pl.ds(first, CHUNK), :] * 0.125
            sine = sine_ref[pl.ds(first, CHUNK), :] * 0.125
            for k in range(heads):
                tiles = []
                for g in range(group_tiles):
                    at = (k * group_tiles + g) * 128
                    tile = query_ref[pl.ds(first, CHUNK), at : at + 128]
                    turned = tile * cosine + swap_halves(tile, chunk_lane) * sine
                    tiles.append(turned.astype(jnp.bfloat16))
                stacked = jnp.concatenate(tiles, axis=0)
                result = None
                for side in range(2):
                    score = lax.dot_general(
                        stacked, tables[k, side], (((1,), (1,)), ((), ())),
                        preferred_element_type=jnp.float32,
                    )
                    score = jnp.where(allowed, score, -jnp.inf)
                    sink = sink_ref[k, :, side : side + 1]
                    largest = jnp.maximum(jnp.max(score, axis=1, keepdims=True), sink)
                    weight = jnp.exp(score - largest)
                    total = jnp.sum(weight, axis=1, keepdims=True) + jnp.exp(sink - largest)
                    weight = (weight * (1.0 / total)).astype(jnp.bfloat16)
                    piece = jnp.dot(weight, tables[k, 2 + side], preferred_element_type=jnp.float32)
                    result = piece if result is None else result + piece
                for g in range(group_tiles):
                    at = (k * group_tiles + g) * 128
                    mixed[pl.ds(first, CHUNK), at : at + 128] = result[g * CHUNK : (g + 1) * CHUNK]
            return carry

        lax.fori_loop(0, (length + CHUNK - 1) // CHUNK, one_chunk, 0)
        return carry

    lax.fori_loop(0, peers, one_request, 0)

    def settle(i, carry):
        at = pl.multiple_of(i * 16, 16)
        out_ref[pl.ds(at, 16), :] = mixed[pl.ds(at, 16), :].astype(jnp.bfloat16)
        return carry

    lax.fori_loop(0, rows // 16, settle, 0)


def attend(queries, paired, cosine, sine, sinks, prefix, home, offsets, starts, lengths):
    peers = starts.shape[0]
    rows, width = queries.shape
    heads = paired.shape[1] // 128
    smem = pl.BlockSpec(memory_space=pltpu.SMEM)
    vmem = pl.BlockSpec(memory_space=pltpu.VMEM)
    return pl.pallas_call(
        attend_kernel,
        out_shape=jax.ShapeDtypeStruct((rows, width), jnp.bfloat16),
        in_specs=[smem] * 4 + [vmem] * 5 + [pl.BlockSpec(memory_space=pl.ANY)],
        out_specs=vmem,
        scratch_shapes=[
            pltpu.VMEM((peers, 2 * WINDOW, heads * 128), jnp.bfloat16),
            pltpu.VMEM((heads, 4, 2 * WINDOW, 128), jnp.bfloat16),
            pltpu.VMEM((rows, width), jnp.float32),
            pltpu.SemaphoreType.DMA((peers, 2)),
        ],
        compiler_params=pltpu.CompilerParams(vmem_limit_bytes=44 * 2**20),
        cost_estimate=pl.CostEstimate(
            flops=rows * width * 2 * WINDOW * 8, bytes_accessed=rows * width * 12,
            transcendentals=rows * width * 4,
        ),
    )(home, offsets, starts, lengths, queries, paired, cosine, sine, sinks, prefix)


def swap(values):
    return lax.ppermute(values, "tp", [(0, 1), (1, 0)])


def local(
    suffix_tokens,
    route_lengths,
    dest_perm,
    attach_points,
    prefix_cache,
    block_of_slot,
    sink_logits,
    attn_gain,
    w_query,
    w_keyval,
    w_out,
    mlp_gain,
    w_gate,
    w_up,
    w_down,
):
    peers = lax.axis_size("req")
    splits = lax.axis_size("tp")
    request_index = lax.axis_index("req")
    tensor_index = lax.axis_index("tp")
    slot_count, slot_length, features = suffix_tokens.shape
    feature_share = features // splits
    slot_share = slot_length // splits
    value_heads = w_keyval.shape[1]
    head_dim = w_keyval.shape[2] // 2
    half_dim = head_dim // 2
    group_tiles = w_query.shape[1] // 128 // value_heads
    row_total = (CAP + (ALIGN - 1) * (peers - 1)) // ALIGN * ALIGN - ALIGN + CHUNK
    peer_ids = jnp.arange(peers)
    slot_steps = jnp.arange(slot_length)
    my_row = lax.dynamic_index_in_dim(dest_perm, request_index, 0, keepdims=False)
    attach_table = attach_points.reshape(peers, peers)
    arriving_lengths = lax.dynamic_index_in_dim(route_lengths, request_index, 0, keepdims=False)
    arriving = (dest_perm == request_index).astype(jnp.int32)
    arriving_attach = jnp.sum(attach_table * arriving, axis=1)
    send_order = jnp.sum(
        jnp.where(my_row[None, :] == peer_ids[:, None], peer_ids[None, :], 0), axis=1
    )
    padded = (arriving_lengths + ALIGN - 1) // ALIGN * ALIGN
    run_ends = jnp.cumsum(padded)
    starts = run_ends - padded
    packed_ids = jnp.arange(row_total)
    source_of = jnp.sum((run_ends[None, :] <= packed_ids[:, None]).astype(jnp.int32), axis=1)
    source_of = jnp.minimum(source_of, peers - 1)
    source_hot = (source_of[:, None] == peer_ids[None, :]).astype(jnp.int32)
    token_index = packed_ids - jnp.sum(source_hot * starts[None, :], axis=1)
    token_index = jnp.minimum(token_index, slot_length - 1)
    positions = jnp.sum(source_hot * arriving_attach[None, :], axis=1) + token_index
    slot_source = jnp.clip(starts[:, None] + slot_steps[None, :], 0, row_total - 1).reshape(-1)
    live_mask = slot_steps[None, :] < arriving_lengths[:, None]

    block_len = prefix_cache.shape[1]
    shelf = prefix_cache.reshape(prefix_cache.shape[0], block_len, -1)
    catalog = jnp.arange(block_of_slot.shape[0])
    home_row = jnp.sum(
        jnp.where(block_of_slot[None, :] == catalog[:, None], catalog[None, :], 0), axis=1
    )
    begin = arriving_attach - WINDOW
    first_block = begin // block_len
    offsets = begin - first_block * block_len
    wanted = jnp.minimum(first_block[:, None] + jnp.arange(2), catalog.shape[0] - 1)
    home = jnp.sum(jnp.where(wanted[..., None] == catalog, home_row, 0), axis=-1)

    share = lax.dynamic_slice_in_dim(suffix_tokens, tensor_index * slot_share, slot_share, 1)
    landed = lax.all_to_all(share[send_order], "req", split_axis=0, concat_axis=0, tiled=True)
    landed, shelf = lax.optimization_barrier((landed, shelf))
    prefix = lax.all_gather(shelf, "req", axis=0, tiled=True)
    part = token_index // slot_share
    within = source_of * slot_share + token_index - part * slot_share
    landed = landed.reshape(peers * slot_share, features)
    if splits == 2:
        mine = landed[within]
        input_rows = jnp.where((part == tensor_index)[:, None], mine, swap(mine))
    else:
        spread = lax.all_gather(landed, "tp", axis=0, tiled=True)
        input_rows = spread[part * (peers * slot_share) + within]
    normed_in = norm_rows(input_rows, attn_gain)
    queries = jnp.dot(normed_in, w_query, preferred_element_type=jnp.float32)
    paired = jnp.dot(
        normed_in, w_keyval.reshape(features, -1), preferred_element_type=jnp.float32
    )
    frequency = ROPE_BASE ** (-(jnp.arange(half_dim).astype(jnp.float32) * 2.0 / head_dim))
    angles = positions.astype(jnp.float32)[:, None] * frequency
    cosine = jnp.tile(jnp.cos(angles), (1, 128 // half_dim))
    sine = jnp.sin(angles)
    sine = jnp.tile(jnp.concatenate([-sine, sine], axis=1), (1, 128 // head_dim))
    sinks = jnp.repeat(sink_logits.reshape(value_heads, group_tiles, 2), CHUNK, axis=1)
    prefix, queries = lax.optimization_barrier((prefix, queries))
    attended = attend(
        queries, paired, cosine, sine, sinks, prefix, home, offsets, starts, arriving_lengths
    )
    partial_value = jnp.dot(attended, w_out, preferred_element_type=jnp.float32).astype(jnp.bfloat16)
    if splits == 2:
        summed = partial_value.astype(jnp.float32) + swap(partial_value).astype(jnp.float32)
    else:
        summed = lax.psum(partial_value, "tp").astype(jnp.float32)
    residual = (input_rows.astype(jnp.float32) + summed).astype(jnp.bfloat16)
    normed_mid = norm_rows(residual, mlp_gain)
    residual_part = lax.dynamic_slice_in_dim(
        residual, tensor_index * feature_share, feature_share, 1
    )
    gate_proj = jnp.dot(normed_mid, w_gate, preferred_element_type=jnp.float32)
    up_proj = jnp.dot(normed_mid, w_up, preferred_element_type=jnp.float32)
    hidden = (jax.nn.silu(gate_proj) * up_proj).astype(jnp.bfloat16)
    down = jnp.dot(hidden, w_down, preferred_element_type=jnp.float32).astype(jnp.bfloat16)
    if splits == 2:
        left, right = down[:, :feature_share], down[:, feature_share:]
        kept = jnp.where(tensor_index == 0, left, right)
        given = swap(jnp.where(tensor_index == 0, right, left))
        down_sum = kept.astype(jnp.float32) + given.astype(jnp.float32)
    else:
        down_sum = lax.psum_scatter(down, "tp", scatter_dimension=1, tiled=True).astype(jnp.float32)
    out_rows = (residual_part.astype(jnp.float32) + down_sum).astype(jnp.bfloat16)
    out_slots = out_rows[slot_source].reshape(peers, slot_length, feature_share)
    out_slots = jnp.where(live_mask[..., None], out_slots, jnp.zeros((), jnp.bfloat16))
    returned = lax.all_to_all(out_slots, "req", split_axis=0, concat_axis=0, tiled=True)
    return returned[my_row]


def solution(mesh):
    in_specs = (
        P("req", None, None),
        P(),
        P(),
        P(),
        P("req", None, "tp", None),
        P(),
        P("tp"),
        P(),
        P(None, "tp"),
        P(None, "tp", None),
        P("tp", None),
        P(),
        P(None, "tp"),
        P(None, "tp"),
        P("tp", None),
    )
    out_specs = P("req", None, "tp")
    return jax.shard_map(local, mesh=mesh, in_specs=in_specs, out_specs=out_specs, check_vma=False)
```

```python
import jax
import jax.numpy as jnp
from jax import lax
from jax.experimental import pallas as pl
from jax.experimental.pallas import tpu as pltpu
from jax.sharding import PartitionSpec as P

WINDOW = 128
CAP = 768


ROPE_BASE = 150000.0
EPSILON = 1e-05


def norm_rows(inputs, gains):
    widened = inputs.astype(jnp.float32)
    factor = lax.rsqrt(jnp.mean(widened * widened, axis=-1, keepdims=True) + EPSILON)
    return (widened * factor * gains.astype(jnp.float32)).astype(jnp.bfloat16)


CHUNK = 32
ALIGN = 8


def swap_halves(tile, lane):
    return jnp.where(lane % 64 < 32, pltpu.roll(tile, 96, 1), pltpu.roll(tile, 32, 1))


def attend_kernel(
    home_ref, offset_ref, start_ref, length_ref,
    query_ref, paired_ref, cosine_ref, sine_ref, sink_ref, prefix_ref,
    out_ref, blocks, tables, mixed, sems,
):
    peers = start_ref.shape[0]
    rows = query_ref.shape[0]
    heads = paired_ref.shape[1] // 128
    group_tiles = query_ref.shape[1] // 128 // heads

    def block_copy(n, half):
        return pltpu.make_async_copy(
            prefix_ref.at[home_ref[n, half]],
            blocks.at[n, pl.ds(half * WINDOW, WINDOW)],
            sems.at[n, half],
        )

    for n in range(peers):
        for half in range(2):
            block_copy(n, half).start()
    mixed[...] = jnp.zeros_like(mixed)

    lane = lax.broadcasted_iota(jnp.int32, (WINDOW, 128), 1)
    low = lane < 64

    def one_request(n, carry):
        start = pl.multiple_of(start_ref[n], ALIGN)
        length = length_ref[n]
        own = pl.multiple_of(jnp.minimum(start, rows - WINDOW), ALIGN)
        block_copy(n, 0).wait()
        block_copy(n, 1).wait()
        shift = (2 * WINDOW - offset_ref[n]) % (2 * WINDOW)
        cosine = cosine_ref[pl.ds(own, WINDOW), :]
        sine = sine_ref[pl.ds(own, WINDOW), :]
        for k in range(heads):
            columns = slice(k * 128, (k + 1) * 128)
            both = blocks[n, :, columns].astype(jnp.float32)
            fetched = pltpu.roll(both, shift, 0)[:WINDOW]
            fresh = paired_ref[pl.ds(own, WINDOW), columns]
            turned = fresh * cosine + swap_halves(fresh, lane) * sine
            fresh = jnp.where(low, turned, fresh)
            for part, tile in enumerate((fetched, fresh)):
                spot = slice(part * WINDOW, (part + 1) * WINDOW)
                moved = pltpu.roll(tile, 64, 1)
                tables[k, 0, spot] = jnp.where(low, tile, 0.0).astype(jnp.bfloat16)
                tables[k, 1, spot] = jnp.where(low, 0.0, moved).astype(jnp.bfloat16)
                tables[k, 2, spot] = jnp.where(low, moved, 0.0).astype(jnp.bfloat16)
                tables[k, 3, spot] = jnp.where(low, 0.0, tile).astype(jnp.bfloat16)

        shape = (group_tiles * CHUNK, 2 * WINDOW)
        step = lax.broadcasted_iota(jnp.int32, shape, 0) % CHUNK
        column = lax.broadcasted_iota(jnp.int32, shape, 1)
        own_step = column - WINDOW + (own - start)
        chunk_lane = lax.broadcasted_iota(jnp.int32, (CHUNK, 128), 1)

        def one_chunk(c, carry):
            first = pl.multiple_of(start + c * CHUNK, ALIGN)
            token = step + c * CHUNK
            allowed = ((column < WINDOW) & (column > token)) | (
                (column >= WINDOW) & (own_step >= 0) & (own_step <= token)
            )
            cosine = cosine_ref[pl.ds(first, CHUNK), :] * 0.125
            sine = sine_ref[pl.ds(first, CHUNK), :] * 0.125
            for k in range(heads):
                tiles = []
                for g in range(group_tiles):
                    at = (k * group_tiles + g) * 128
                    tile = query_ref[pl.ds(first, CHUNK), at : at + 128]
                    turned = tile * cosine + swap_halves(tile, chunk_lane) * sine
                    tiles.append(turned.astype(jnp.bfloat16))
                stacked = jnp.concatenate(tiles, axis=0)
                result = None
                for side in range(2):
                    score = lax.dot_general(
                        stacked, tables[k, side], (((1,), (1,)), ((), ())),
                        preferred_element_type=jnp.float32,
                    )
                    score = jnp.where(allowed, score, -jnp.inf)
                    sink = sink_ref[k, :, side : side + 1]
                    largest = jnp.maximum(jnp.max(score, axis=1, keepdims=True), sink)
                    weight = jnp.exp(score - largest)
                    total = jnp.sum(weight, axis=1, keepdims=True) + jnp.exp(sink - largest)
                    piece = jnp.dot(
                        weight.astype(jnp.bfloat16), tables[k, 2 + side],
                        preferred_element_type=jnp.float32,
                    ) * (1.0 / total)
                    result = piece if result is None else result + piece
                for g in range(group_tiles):
                    at = (k * group_tiles + g) * 128
                    mixed[pl.ds(first, CHUNK), at : at + 128] = result[g * CHUNK : (g + 1) * CHUNK]
            return carry

        lax.fori_loop(0, (length + CHUNK - 1) // CHUNK, one_chunk, 0)
        return carry

    lax.fori_loop(0, peers, one_request, 0)

    def settle(i, carry):
        at = pl.multiple_of(i * 16, 16)
        out_ref[pl.ds(at, 16), :] = mixed[pl.ds(at, 16), :].astype(jnp.bfloat16)
        return carry

    lax.fori_loop(0, rows // 16, settle, 0)


def attend(queries, paired, cosine, sine, sinks, prefix, home, offsets, starts, lengths):
    peers = starts.shape[0]
    rows, width = queries.shape
    heads = paired.shape[1] // 128
    smem = pl.BlockSpec(memory_space=pltpu.SMEM)
    vmem = pl.BlockSpec(memory_space=pltpu.VMEM)
    return pl.pallas_call(
        attend_kernel,
        out_shape=jax.ShapeDtypeStruct((rows, width), jnp.bfloat16),
        in_specs=[smem] * 4 + [vmem] * 5 + [pl.BlockSpec(memory_space=pl.ANY)],
        out_specs=vmem,
        scratch_shapes=[
            pltpu.VMEM((peers, 2 * WINDOW, heads * 128), jnp.bfloat16),
            pltpu.VMEM((heads, 4, 2 * WINDOW, 128), jnp.bfloat16),
            pltpu.VMEM((rows, width), jnp.float32),
            pltpu.SemaphoreType.DMA((peers, 2)),
        ],
        compiler_params=pltpu.CompilerParams(vmem_limit_bytes=44 * 2**20),
        cost_estimate=pl.CostEstimate(
            flops=rows * width * 2 * WINDOW * 8, bytes_accessed=rows * width * 12,
            transcendentals=rows * width * 4,
        ),
    )(home, offsets, starts, lengths, queries, paired, cosine, sine, sinks, prefix)


def pack_kernel(start_ref, core_ref, mine_ref, other_ref, gain_ref, rows_ref, normed_ref, held):
    n = pl.program_id(0)
    share = mine_ref.shape[1]
    start = pl.multiple_of(start_ref[n], ALIGN)
    near = pl.multiple_of(start + core_ref[0] * share, ALIGN)
    far = pl.multiple_of(start + (1 - core_ref[0]) * share, ALIGN)

    @pl.when(n == 0)
    def _():
        def clear(i, carry):
            at = pl.multiple_of(i * ALIGN, ALIGN)
            held[pl.ds(at, ALIGN), :] = jnp.zeros((ALIGN, held.shape[1]), jnp.float32)
            return carry

        lax.fori_loop(0, held.shape[0] // ALIGN, clear, 0)

    held[pl.ds(near, share), :] = mine_ref[0].astype(jnp.float32)
    held[pl.ds(far, share), :] = other_ref[0].astype(jnp.float32)

    @pl.when(n == pl.num_programs(0) - 1)
    def _():
        def settle(i, carry):
            at = pl.multiple_of(i * 16, 16)
            tile = held[pl.ds(at, 16), :]
            factor = lax.rsqrt(jnp.mean(tile * tile, axis=1, keepdims=True) + EPSILON)
            rows_ref[pl.ds(at, 16), :] = tile.astype(jnp.bfloat16)
            normed_ref[pl.ds(at, 16), :] = (tile * factor * gain_ref[...]).astype(jnp.bfloat16)
            return carry

        lax.fori_loop(0, rows_ref.shape[0] // 16, settle, 0)


def pack(mine, other, starts, tensor_index, gains, row_total):
    peers, share, features = mine.shape
    smem = pl.BlockSpec(memory_space=pltpu.SMEM)
    half = pl.BlockSpec((1, share, features), lambda n: (n, 0, 0))
    whole = pl.BlockSpec((row_total, features), lambda n: (0, 0))
    return pl.pallas_call(
        pack_kernel,
        grid=(peers,),
        out_shape=[jax.ShapeDtypeStruct((row_total, features), jnp.bfloat16)] * 2,
        in_specs=[smem, smem, half, half, pl.BlockSpec((1, features), lambda n: (0, 0))],
        out_specs=[whole, whole],
        scratch_shapes=[pltpu.VMEM((row_total + 2 * share, features), jnp.float32)],
        compiler_params=pltpu.CompilerParams(vmem_limit_bytes=44 * 2**20),
    )(starts, tensor_index.reshape(1), mine, other, gains.astype(jnp.float32).reshape(1, -1))


def unpack_kernel(start_ref, length_ref, residual_ref, kept_ref, given_ref, out_ref, held):
    n = pl.program_id(0)
    rows = residual_ref.shape[0]
    slots, width = out_ref.shape[1:]

    @pl.when(n == 0)
    def _():
        def settle(i, carry):
            at = pl.multiple_of(i * 16, 16)
            spot = pl.ds(at, 16)
            moved = kept_ref[spot, :].astype(jnp.float32) + given_ref[spot, :].astype(jnp.float32)
            held[spot, :] = residual_ref[spot, :].astype(jnp.float32) + moved
            return carry

        lax.fori_loop(0, rows // 16, settle, 0)

    step = lax.broadcasted_iota(jnp.int32, (slots, width), 0)
    tile = held[pl.ds(pl.multiple_of(start_ref[n], ALIGN), slots), :]
    out_ref[0] = jnp.where(step < length_ref[n], tile, 0.0).astype(jnp.bfloat16)


def unpack(residual, kept, given, starts, lengths, slot_length):
    peers = starts.shape[0]
    rows, width = residual.shape
    smem = pl.BlockSpec(memory_space=pltpu.SMEM)
    whole = pl.BlockSpec((rows, width), lambda n: (0, 0))
    return pl.pallas_call(
        unpack_kernel,
        grid=(peers,),
        out_shape=jax.ShapeDtypeStruct((peers, slot_length, width), jnp.bfloat16),
        in_specs=[smem, smem, whole, whole, whole],
        out_specs=pl.BlockSpec((1, slot_length, width), lambda n: (n, 0, 0)),
        scratch_shapes=[pltpu.VMEM((rows + slot_length, width), jnp.float32)],
        compiler_params=pltpu.CompilerParams(vmem_limit_bytes=44 * 2**20),
    )(starts, lengths, residual, kept, given)


def swap(values):
    return lax.ppermute(values, "tp", [(0, 1), (1, 0)])


def local(
    suffix_tokens,
    route_lengths,
    dest_perm,
    attach_points,
    prefix_cache,
    block_of_slot,
    sink_logits,
    attn_gain,
    w_query,
    w_keyval,
    w_out,
    mlp_gain,
    w_gate,
    w_up,
    w_down,
):
    peers = lax.axis_size("req")
    splits = lax.axis_size("tp")
    request_index = lax.axis_index("req")
    tensor_index = lax.axis_index("tp")
    slot_count, slot_length, features = suffix_tokens.shape
    feature_share = features // splits
    slot_share = slot_length // splits
    value_heads = w_keyval.shape[1]
    head_dim = w_keyval.shape[2] // 2
    half_dim = head_dim // 2
    group_tiles = w_query.shape[1] // 128 // value_heads
    row_total = (CAP + (ALIGN - 1) * (peers - 1)) // ALIGN * ALIGN - ALIGN + CHUNK
    peer_ids = jnp.arange(peers)
    slot_steps = jnp.arange(slot_length)
    my_row = lax.dynamic_index_in_dim(dest_perm, request_index, 0, keepdims=False)
    attach_table = attach_points.reshape(peers, peers)
    arriving_lengths = lax.dynamic_index_in_dim(route_lengths, request_index, 0, keepdims=False)
    arriving = (dest_perm == request_index).astype(jnp.int32)
    arriving_attach = jnp.sum(attach_table * arriving, axis=1)
    send_order = jnp.sum(
        jnp.where(my_row[None, :] == peer_ids[:, None], peer_ids[None, :], 0), axis=1
    )
    padded = (arriving_lengths + ALIGN - 1) // ALIGN * ALIGN
    run_ends = jnp.cumsum(padded)
    starts = run_ends - padded
    packed_ids = jnp.arange(row_total)
    source_of = jnp.sum((run_ends[None, :] <= packed_ids[:, None]).astype(jnp.int32), axis=1)
    source_of = jnp.minimum(source_of, peers - 1)
    source_hot = (source_of[:, None] == peer_ids[None, :]).astype(jnp.int32)
    token_index = packed_ids - jnp.sum(source_hot * starts[None, :], axis=1)
    token_index = jnp.minimum(token_index, slot_length - 1)
    positions = jnp.sum(source_hot * arriving_attach[None, :], axis=1) + token_index
    slot_source = jnp.clip(starts[:, None] + slot_steps[None, :], 0, row_total - 1).reshape(-1)
    live_mask = slot_steps[None, :] < arriving_lengths[:, None]

    block_len = prefix_cache.shape[1]
    shelf = prefix_cache.reshape(prefix_cache.shape[0], block_len, -1)
    catalog = jnp.arange(block_of_slot.shape[0])
    home_row = jnp.sum(
        jnp.where(block_of_slot[None, :] == catalog[:, None], catalog[None, :], 0), axis=1
    )
    begin = arriving_attach - WINDOW
    first_block = begin // block_len
    offsets = begin - first_block * block_len
    wanted = jnp.minimum(first_block[:, None] + jnp.arange(2), catalog.shape[0] - 1)
    home = jnp.sum(jnp.where(wanted[..., None] == catalog, home_row, 0), axis=-1)

    share = lax.dynamic_slice_in_dim(suffix_tokens, tensor_index * slot_share, slot_share, 1)
    landed = lax.all_to_all(share[send_order], "req", split_axis=0, concat_axis=0, tiled=True)
    prefix = lax.all_gather(shelf, "req", axis=0, tiled=True)
    part = token_index // slot_share
    within = source_of * slot_share + token_index - part * slot_share
    if splits == 2:
        input_rows, normed_in = pack(
            landed, swap(landed), starts, tensor_index, attn_gain, row_total
        )
    else:
        landed = landed.reshape(peers * slot_share, features)
        spread = lax.all_gather(landed, "tp", axis=0, tiled=True)
        input_rows = spread[part * (peers * slot_share) + within]
        normed_in = norm_rows(input_rows, attn_gain)
    queries = jnp.dot(normed_in, w_query, preferred_element_type=jnp.float32)
    paired = jnp.dot(
        normed_in, w_keyval.reshape(features, -1), preferred_element_type=jnp.float32
    )
    frequency = ROPE_BASE ** (-(jnp.arange(half_dim).astype(jnp.float32) * 2.0 / head_dim))
    angles = positions.astype(jnp.float32)[:, None] * frequency
    cosine = jnp.tile(jnp.cos(angles), (1, 128 // half_dim))
    sine = jnp.sin(angles)
    sine = jnp.tile(jnp.concatenate([-sine, sine], axis=1), (1, 128 // head_dim))
    sinks = jnp.repeat(sink_logits.reshape(value_heads, group_tiles, 2), CHUNK, axis=1)
    prefix, queries = lax.optimization_barrier((prefix, queries))
    attended = attend(
        queries, paired, cosine, sine, sinks, prefix, home, offsets, starts, arriving_lengths
    )
    partial_value = jnp.dot(attended, w_out, preferred_element_type=jnp.float32).astype(jnp.bfloat16)
    if splits == 2:
        summed = partial_value.astype(jnp.float32) + swap(partial_value).astype(jnp.float32)
    else:
        summed = lax.psum(partial_value, "tp").astype(jnp.float32)
    residual = (input_rows.astype(jnp.float32) + summed).astype(jnp.bfloat16)
    normed_mid = norm_rows(residual, mlp_gain)
    residual_part = lax.dynamic_slice_in_dim(
        residual, tensor_index * feature_share, feature_share, 1
    )
    gate_proj = jnp.dot(normed_mid, w_gate, preferred_element_type=jnp.float32)
    up_proj = jnp.dot(normed_mid, w_up, preferred_element_type=jnp.float32)
    hidden = (jax.nn.silu(gate_proj) * up_proj).astype(jnp.bfloat16)
    down = jnp.dot(hidden, w_down, preferred_element_type=jnp.float32).astype(jnp.bfloat16)
    if splits == 2:
        left, right = down[:, :feature_share], down[:, feature_share:]
        kept = jnp.where(tensor_index == 0, left, right)
        given = swap(jnp.where(tensor_index == 0, right, left))
        out_slots = unpack(residual_part, kept, given, starts, arriving_lengths, slot_length)
    else:
        down_sum = lax.psum_scatter(down, "tp", scatter_dimension=1, tiled=True).astype(jnp.float32)
        out_rows = (residual_part.astype(jnp.float32) + down_sum).astype(jnp.bfloat16)
        out_slots = out_rows[slot_source].reshape(peers, slot_length, feature_share)
        out_slots = jnp.where(live_mask[..., None], out_slots, jnp.zeros((), jnp.bfloat16))
    returned = lax.all_to_all(out_slots, "req", split_axis=0, concat_axis=0, tiled=True)
    return returned[my_row]


def solution(mesh):
    in_specs = (
        P("req", None, None),
        P(),
        P(),
        P(),
        P("req", None, "tp", None),
        P(),
        P("tp"),
        P(),
        P(None, "tp"),
        P(None, "tp", None),
        P("tp", None),
        P(),
        P(None, "tp"),
        P(None, "tp"),
        P("tp", None),
    )
    out_specs = P("req", None, "tp")
    return jax.shard_map(local, mesh=mesh, in_specs=in_specs, out_specs=out_specs, check_vma=False)
```

```python
import jax
import jax.numpy as jnp
from jax import lax
from jax.experimental import pallas as pl
from jax.experimental.pallas import tpu as pltpu
from jax.sharding import PartitionSpec as P

WINDOW = 128
CAP = 768


ROPE_BASE = 150000.0
EPSILON = 1e-05


def norm_rows(inputs, gains):
    widened = inputs.astype(jnp.float32)
    factor = lax.rsqrt(jnp.mean(widened * widened, axis=-1, keepdims=True) + EPSILON)
    return (widened * factor * gains.astype(jnp.float32)).astype(jnp.bfloat16)


CHUNK = 32
ALIGN = 8


def swap_halves(tile, lane):
    return jnp.where(lane % 64 < 32, pltpu.roll(tile, 96, 1), pltpu.roll(tile, 32, 1))


def attend_kernel(
    home_ref, offset_ref, start_ref, length_ref,
    query_ref, paired_ref, cosine_ref, sine_ref, sink_ref, prefix_ref,
    out_ref, blocks, tables, mixed, sems,
):
    peers = start_ref.shape[0]
    rows = query_ref.shape[0]
    heads = paired_ref.shape[1] // 128
    group_tiles = query_ref.shape[1] // 128 // heads

    def block_copy(n, half):
        return pltpu.make_async_copy(
            prefix_ref.at[home_ref[n, half]],
            blocks.at[n, pl.ds(half * WINDOW, WINDOW)],
            sems.at[n, half],
        )

    for n in range(peers):
        for half in range(2):
            block_copy(n, half).start()
    mixed[...] = jnp.zeros_like(mixed)

    lane = lax.broadcasted_iota(jnp.int32, (WINDOW, 128), 1)
    low = lane < 64

    def one_request(n, carry):
        start = pl.multiple_of(start_ref[n], ALIGN)
        length = length_ref[n]
        own = pl.multiple_of(jnp.minimum(start, rows - WINDOW), ALIGN)
        block_copy(n, 0).wait()
        block_copy(n, 1).wait()
        shift = (2 * WINDOW - offset_ref[n]) % (2 * WINDOW)
        cosine = cosine_ref[pl.ds(own, WINDOW), :]
        sine = sine_ref[pl.ds(own, WINDOW), :]
        for k in range(heads):
            columns = slice(k * 128, (k + 1) * 128)
            both = blocks[n, :, columns].astype(jnp.float32)
            fetched = pltpu.roll(both, shift, 0)[:WINDOW]
            fresh = paired_ref[pl.ds(own, WINDOW), columns]
            turned = fresh * cosine + swap_halves(fresh, lane) * sine
            fresh = jnp.where(low, turned, fresh)
            for part, tile in enumerate((fetched, fresh)):
                spot = slice(part * WINDOW, (part + 1) * WINDOW)
                moved = pltpu.roll(tile, 64, 1)
                tables[k, 0, spot] = jnp.where(low, tile, 0.0).astype(jnp.bfloat16)
                tables[k, 1, spot] = jnp.where(low, 0.0, moved).astype(jnp.bfloat16)
                tables[k, 2, spot] = jnp.where(low, moved, 0.0).astype(jnp.bfloat16)
                tables[k, 3, spot] = jnp.where(low, 0.0, tile).astype(jnp.bfloat16)

        shape = (group_tiles * CHUNK, 2 * WINDOW)
        step = lax.broadcasted_iota(jnp.int32, shape, 0) % CHUNK
        column = lax.broadcasted_iota(jnp.int32, shape, 1)
        own_step = column - WINDOW + (own - start)
        chunk_lane = lax.broadcasted_iota(jnp.int32, (CHUNK, 128), 1)

        def one_chunk(c, carry):
            first = pl.multiple_of(start + c * CHUNK, ALIGN)
            token = step + c * CHUNK
            allowed = ((column < WINDOW) & (column > token)) | (
                (column >= WINDOW) & (own_step >= 0) & (own_step <= token)
            )
            cosine = cosine_ref[pl.ds(first, CHUNK), :] * 0.125
            sine = sine_ref[pl.ds(first, CHUNK), :] * 0.125
            for k in range(heads):
                tiles = []
                for g in range(group_tiles):
                    at = (k * group_tiles + g) * 128
                    tile = query_ref[pl.ds(first, CHUNK), at : at + 128]
                    turned = tile * cosine + swap_halves(tile, chunk_lane) * sine
                    tiles.append(turned.astype(jnp.bfloat16))
                stacked = jnp.concatenate(tiles, axis=0)
                result = None
                for side in range(2):
                    score = lax.dot_general(
                        stacked, tables[k, side], (((1,), (1,)), ((), ())),
                        preferred_element_type=jnp.float32,
                    )
                    score = jnp.where(allowed, score, -jnp.inf)
                    sink = sink_ref[k, :, side : side + 1]
                    largest = jnp.maximum(jnp.max(score, axis=1, keepdims=True), sink)
                    weight = jnp.exp(score - largest)
                    total = jnp.sum(weight, axis=1, keepdims=True) + jnp.exp(sink - largest)
                    weight = (weight * (1.0 / total)).astype(jnp.bfloat16)
                    piece = jnp.dot(weight, tables[k, 2 + side], preferred_element_type=jnp.float32)
                    result = piece if result is None else result + piece
                for g in range(group_tiles):
                    at = (k * group_tiles + g) * 128
                    mixed[pl.ds(first, CHUNK), at : at + 128] = result[g * CHUNK : (g + 1) * CHUNK]
            return carry

        lax.fori_loop(0, (length + CHUNK - 1) // CHUNK, one_chunk, 0)
        return carry

    lax.fori_loop(0, peers, one_request, 0)

    def settle(i, carry):
        at = pl.multiple_of(i * 16, 16)
        out_ref[pl.ds(at, 16), :] = mixed[pl.ds(at, 16), :].astype(jnp.bfloat16)
        return carry

    lax.fori_loop(0, rows // 16, settle, 0)


def attend(queries, paired, cosine, sine, sinks, prefix, home, offsets, starts, lengths):
    peers = starts.shape[0]
    rows, width = queries.shape
    heads = paired.shape[1] // 128
    smem = pl.BlockSpec(memory_space=pltpu.SMEM)
    vmem = pl.BlockSpec(memory_space=pltpu.VMEM)
    return pl.pallas_call(
        attend_kernel,
        out_shape=jax.ShapeDtypeStruct((rows, width), jnp.bfloat16),
        in_specs=[smem] * 4 + [vmem] * 5 + [pl.BlockSpec(memory_space=pl.ANY)],
        out_specs=vmem,
        scratch_shapes=[
            pltpu.VMEM((peers, 2 * WINDOW, heads * 128), jnp.bfloat16),
            pltpu.VMEM((heads, 4, 2 * WINDOW, 128), jnp.bfloat16),
            pltpu.VMEM((rows, width), jnp.float32),
            pltpu.SemaphoreType.DMA((peers, 2)),
        ],
        compiler_params=pltpu.CompilerParams(vmem_limit_bytes=44 * 2**20),
        cost_estimate=pl.CostEstimate(
            flops=rows * width * 2 * WINDOW * 8, bytes_accessed=rows * width * 12,
            transcendentals=rows * width * 4,
        ),
    )(home, offsets, starts, lengths, queries, paired, cosine, sine, sinks, prefix)


def swap(values):
    return lax.ppermute(values, "tp", [(0, 1), (1, 0)])


def local(
    suffix_tokens,
    route_lengths,
    dest_perm,
    attach_points,
    prefix_cache,
    block_of_slot,
    sink_logits,
    attn_gain,
    w_query,
    w_keyval,
    w_out,
    mlp_gain,
    w_gate,
    w_up,
    w_down,
):
    peers = lax.axis_size("req")
    splits = lax.axis_size("tp")
    request_index = lax.axis_index("req")
    tensor_index = lax.axis_index("tp")
    slot_count, slot_length, features = suffix_tokens.shape
    feature_share = features // splits
    slot_share = slot_length // splits
    value_heads = w_keyval.shape[1]
    head_dim = w_keyval.shape[2] // 2
    half_dim = head_dim // 2
    group_tiles = w_query.shape[1] // 128 // value_heads
    row_total = (CAP + (ALIGN - 1) * (peers - 1)) // ALIGN * ALIGN - ALIGN + CHUNK
    peer_ids = jnp.arange(peers)
    slot_steps = jnp.arange(slot_length)
    my_row = lax.dynamic_index_in_dim(dest_perm, request_index, 0, keepdims=False)
    attach_table = attach_points.reshape(peers, peers)
    arriving_lengths = lax.dynamic_index_in_dim(route_lengths, request_index, 0, keepdims=False)
    arriving = (dest_perm == request_index).astype(jnp.int32)
    arriving_attach = jnp.sum(attach_table * arriving, axis=1)
    send_order = jnp.sum(
        jnp.where(my_row[None, :] == peer_ids[:, None], peer_ids[None, :], 0), axis=1
    )
    padded = (arriving_lengths + ALIGN - 1) // ALIGN * ALIGN
    run_ends = jnp.cumsum(padded)
    starts = run_ends - padded
    packed_ids = jnp.arange(row_total)
    source_of = jnp.sum((run_ends[None, :] <= packed_ids[:, None]).astype(jnp.int32), axis=1)
    source_of = jnp.minimum(source_of, peers - 1)
    source_hot = (source_of[:, None] == peer_ids[None, :]).astype(jnp.int32)
    token_index = packed_ids - jnp.sum(source_hot * starts[None, :], axis=1)
    token_index = jnp.minimum(token_index, slot_length - 1)
    positions = jnp.sum(source_hot * arriving_attach[None, :], axis=1) + token_index
    slot_source = jnp.clip(starts[:, None] + slot_steps[None, :], 0, row_total - 1).reshape(-1)
    live_mask = slot_steps[None, :] < arriving_lengths[:, None]

    block_len = prefix_cache.shape[1]
    shelf = prefix_cache.reshape(prefix_cache.shape[0], block_len, -1)
    catalog = jnp.arange(block_of_slot.shape[0])
    home_row = jnp.sum(
        jnp.where(block_of_slot[None, :] == catalog[:, None], catalog[None, :], 0), axis=1
    )
    begin = arriving_attach - WINDOW
    first_block = begin // block_len
    offsets = begin - first_block * block_len
    wanted = jnp.minimum(first_block[:, None] + jnp.arange(2), catalog.shape[0] - 1)
    home = jnp.sum(jnp.where(wanted[..., None] == catalog, home_row, 0), axis=-1)

    share = lax.dynamic_slice_in_dim(suffix_tokens, tensor_index * slot_share, slot_share, 1)
    landed = lax.all_to_all(share[send_order], "req", split_axis=0, concat_axis=0, tiled=True)
    prefix = lax.all_gather(shelf, "req", axis=0, tiled=True)
    part = token_index // slot_share
    within = source_of * slot_share + token_index - part * slot_share
    landed = landed.reshape(peers * slot_share, features)
    if splits == 2:
        mine = landed[within]
        input_rows = jnp.where((part == tensor_index)[:, None], mine, swap(mine))
    else:
        spread = lax.all_gather(landed, "tp", axis=0, tiled=True)
        input_rows = spread[part * (peers * slot_share) + within]
    normed_in = norm_rows(input_rows, attn_gain)
    queries = jnp.dot(normed_in, w_query, preferred_element_type=jnp.float32)
    paired = jnp.dot(
        normed_in, w_keyval.reshape(features, -1), preferred_element_type=jnp.float32
    )
    frequency = ROPE_BASE ** (-(jnp.arange(half_dim).astype(jnp.float32) * 2.0 / head_dim))
    angles = positions.astype(jnp.float32)[:, None] * frequency
    cosine = jnp.tile(jnp.cos(angles), (1, 128 // half_dim))
    sine = jnp.sin(angles)
    sine = jnp.tile(jnp.concatenate([-sine, sine], axis=1), (1, 128 // head_dim))
    sinks = jnp.repeat(sink_logits.reshape(value_heads, group_tiles, 2), CHUNK, axis=1)
    prefix, queries = lax.optimization_barrier((prefix, queries))
    attended = attend(
        queries, paired, cosine, sine, sinks, prefix, home, offsets, starts, arriving_lengths
    )
    partial_value = jnp.dot(attended, w_out, preferred_element_type=jnp.float32).astype(jnp.bfloat16)
    if splits == 2:
        summed = partial_value.astype(jnp.float32) + swap(partial_value).astype(jnp.float32)
    else:
        summed = lax.psum(partial_value, "tp").astype(jnp.float32)
    residual = (input_rows.astype(jnp.float32) + summed).astype(jnp.bfloat16)
    normed_mid = norm_rows(residual, mlp_gain)
    residual_part = lax.dynamic_slice_in_dim(
        residual, tensor_index * feature_share, feature_share, 1
    )
    gate_proj = jnp.dot(normed_mid, w_gate, preferred_element_type=jnp.float32)
    up_proj = jnp.dot(normed_mid, w_up, preferred_element_type=jnp.float32)
    hidden = (jax.nn.silu(gate_proj) * up_proj).astype(jnp.bfloat16)
    down = jnp.dot(hidden, w_down, preferred_element_type=jnp.float32).astype(jnp.bfloat16)
    if splits == 2:
        left, right = down[:, :feature_share], down[:, feature_share:]
        kept = jnp.where(tensor_index == 0, left, right)
        given = swap(jnp.where(tensor_index == 0, right, left))
        down_sum = kept.astype(jnp.float32) + given.astype(jnp.float32)
    else:
        down_sum = lax.psum_scatter(down, "tp", scatter_dimension=1, tiled=True).astype(jnp.float32)
    out_rows = (residual_part.astype(jnp.float32) + down_sum).astype(jnp.bfloat16)
    out_slots = out_rows[slot_source].reshape(peers, slot_length, feature_share)
    out_slots = jnp.where(live_mask[..., None], out_slots, jnp.zeros((), jnp.bfloat16))
    returned = lax.all_to_all(out_slots, "req", split_axis=0, concat_axis=0, tiled=True)
    return returned[my_row]


def solution(mesh):
    in_specs = (
        P("req", None, None),
        P(),
        P(),
        P(),
        P("req", None, "tp", None),
        P(),
        P("tp"),
        P(),
        P(None, "tp"),
        P(None, "tp", None),
        P("tp", None),
        P(),
        P(None, "tp"),
        P(None, "tp"),
        P("tp", None),
    )
    out_specs = P("req", None, "tp")
    return jax.shard_map(local, mesh=mesh, in_specs=in_specs, out_specs=out_specs, check_vma=False)
```
